128 devices in a mesh: dp: 32 (over x, z, core), mp: 4 (over y).
Axes of the slice: x: 4, y: 4, z: 4, core: 2. Of those that a mesh axis runs over, the one named last changes fastest.
Arguments:
- block_states: bfloat16 [64, 128, 4096], P('dp', None, 'mp'), may hold values from -6 to 6
- norm_gain: bfloat16 [4096], P('mp'), may hold values from 0.099609375 to 1.8984375
- key_weight: bfloat16 [4096, 4096], P(None, 'mp'), may hold values from -0.09375 to 0.09375
- value_weight: bfloat16 [4096, 4096], P(None, 'mp'), may hold values from -0.09375 to 0.09375
- queries: bfloat16 [8192, 4096], P('dp', 'mp'), may hold values from -21 to 21
- wanted: int32 [32, 32], replicated, may hold values from -1 to 1, as said below
Outputs:
- attended: bfloat16 [8192, 4096], P('dp', 'mp')
The draws below stay inside these ranges and needn't reach their ends.
Inputs may be any that keep to these rules, and one draw needn't show every extreme that they name: `wanted`: each question reads from between 8 and 24 encoder indices, at most one block from each; some question reads from exactly 24.
All inputs are finite; a program needn't handle non-finite values.
Results may differ from the reference program's by a relative error of at most 0.0065.
The reference program's roundings to bfloat16 on the way (of `normed` and `probs`) count: a program that leaves them out, or rounds other values in their place, can miss the bound.
Values may be sent and summed in bfloat16 or wider, within the bound.
No kernel may reach another device: no remote copies, remote signals or barrier semaphores. Data moves between devices by JAX's collectives and lax.ppermute only.
A program may use at most 128 MiB of HBM per device.

```python
import jax
import jax.numpy as jnp
from jax import lax

D = 4096
HD = 64
HEADS = 64
BLOCK = 128
BLK_DEV = 2
QTOK = 256
QUESTIONS = 32
NBLK = 64
MINREF = 8
MAXREF = 24


def draw_queries(key, part):
    key = jax.random.fold_in(key, 5)
    first_key = jax.random.fold_in(key, 0)
    values = 0.35 * jnp.clip(jax.random.normal(first_key, (QUESTIONS * QTOK, D), jnp.float32), -6.0, 6.0)
    return values.astype(jnp.bfloat16)


def draw_wanted(key, part):
    key = jax.random.fold_in(key, 11)
    order_key, count_key, block_key = jax.random.split(key, 3)
    order_keys = jax.random.split(order_key, QUESTIONS)
    orders = jax.vmap(lambda single: jax.random.permutation(single, QUESTIONS))(order_keys)
    counts = jax.random.randint(count_key, (QUESTIONS,), MINREF, MAXREF + 1)
    counts = jnp.where(jnp.arange(QUESTIONS) == 0, MAXREF, counts)
    chosen_block = jax.random.randint(block_key, (QUESTIONS, QUESTIONS), 0, BLK_DEV)
    return jnp.where(orders < counts[:, None], chosen_block, -1).astype(jnp.int32)


def level_of(own_key, extent, shards, smallest, top_value):
    gain, own = 1.0, jax.random.fold_in(own_key, 6)
    for position, parts in shards:
        draws = jnp.exp(jax.random.uniform(jax.random.fold_in(own, position), (parts,), jnp.float32, smallest / len(shards), top_value / len(shards)))
        gain = gain * jnp.repeat(draws, extent[position] // parts).reshape([-1 if axis == position else 1 for axis in range(len(extent))])
    return gain


def normal_values(rng, dims, spread, reach, cuts=(), kind=jnp.bfloat16):
    values = spread * jax.random.normal(rng, dims, jnp.float32)
    if cuts:
        values = values * level_of(rng, dims, cuts, -0.22, 0.18)
    return jnp.clip(values, -reach, reach).astype(kind)


def setup_inputs(seed: int = 0) -> dict:
    key_list = jax.random.split(jax.random.key(seed), 7)
    block_states = normal_values(key_list[0], (NBLK, BLOCK, D), 1.0, 6.0, ((0, 32), (2, 4)))
    norm_gain = jnp.clip(1.0 + 0.18 * jax.random.normal(key_list[1], (D,), jnp.float32), 0.099609375, 1.8984375).astype(jnp.bfloat16)
    key_weight = normal_values(key_list[2], (D, D), D ** -0.5, 0.09375, ((1, 4),))
    value_weight = normal_values(key_list[3], (D, D), D ** -0.5, 0.09375, ((1, 4),))
    queries = draw_queries(jax.random.fold_in(key_list[6], 71), 0)
    wanted = draw_wanted(jax.random.fold_in(key_list[6], 71), 0)
    return {"block_states": block_states, "norm_gain": norm_gain, "key_weight": key_weight, "value_weight": value_weight, "queries": queries, "wanted": wanted}


def reference(block_states, norm_gain, key_weight, value_weight, queries, wanted):
    floats = block_states.astype(jnp.float32)
    mean_square = lax.optimization_barrier(jnp.mean(floats * floats, axis=-1, keepdims=True))
    normed = (floats * lax.rsqrt(mean_square + 1e-06) * norm_gain.astype(jnp.float32)).astype(jnp.bfloat16)
    flat_rows = normed.reshape(-1, D)
    all_keys = jnp.dot(flat_rows, key_weight, preferred_element_type=jnp.float32).astype(jnp.bfloat16)
    all_values = jnp.dot(flat_rows, value_weight, preferred_element_type=jnp.float32).astype(jnp.bfloat16)
    all_keys = all_keys.reshape(-1, BLOCK, D)
    all_values = all_values.reshape(-1, BLOCK, D)
    devices = jnp.arange(QUESTIONS, dtype=jnp.int32)

    def per_question(question):
        wanted_row = lax.dynamic_index_in_dim(wanted, question, 0, keepdims=False)
        block_ids = (devices * BLK_DEV + jnp.maximum(wanted_row, 0)).astype(jnp.int32)
        key_rows = jnp.take(all_keys, block_ids, axis=0).reshape(-1, HEADS, HD).astype(jnp.float32)
        value_rows = jnp.take(all_values, block_ids, axis=0).reshape(-1, HEADS, HD).astype(jnp.float32)
        usable = jnp.repeat(wanted_row >= 0, BLOCK)
        start_row = (question * QTOK).astype(jnp.int32)
        query_rows = lax.dynamic_slice_in_dim(queries, start_row, QTOK, 0)
        query_rows = query_rows.reshape(QTOK, HEADS, HD).astype(jnp.float32)

        def per_head(triple):
            query_head, key_head, value_head = triple
            scores = jnp.dot(query_head, key_head.T)
            scores = jnp.where(usable[None, :], scores, -1e+30)
            top_score = lax.optimization_barrier(jnp.max(scores, axis=-1, keepdims=True))
            probs = jnp.where(usable[None, :], jnp.exp(scores - top_score), 0.0).astype(jnp.bfloat16)
            prob_floats = probs.astype(jnp.float32)
            denominator = lax.optimization_barrier(jnp.sum(prob_floats, axis=-1, keepdims=True))
            return jnp.dot(prob_floats, value_head) / denominator
        results = lax.map(per_head, (query_rows.transpose(1, 0, 2), key_rows.transpose(1, 0, 2), value_rows.transpose(1, 0, 2)))
        return results.transpose(1, 0, 2).reshape(QTOK, D).astype(jnp.bfloat16)
    return lax.map(per_question, devices).reshape(QUESTIONS * QTOK, D)
```

```python
import functools

import jax
import jax.numpy as jnp
from jax import lax
from jax.experimental import pallas as pl
from jax.experimental.pallas import tpu as pltpu
from jax.sharding import PartitionSpec as P

AXES = ("dp", "mp")
SIDE = 4
HD = 64
BLOCK = 128
HALF = 512
PAIRS = 4
TILE = 128
QTOK = 256
STAT = 32
OFFSETS = (0, 3, 1, 2)
F32, BF16 = jnp.float32, jnp.bfloat16


def device_id(x, y, z, c):
    return ((x * SIDE + z) * 2 + c) * SIDE + y


def permutation(move):
    pairs = []
    for x in range(SIDE):
        for z in range(SIDE):
            for c in range(2):
                for y in range(SIDE):
                    pairs.append((device_id(x, y, z, c), device_id(*move(x, y, z, c))))
    return pairs


def along_y(step):
    return permutation(lambda x, y, z, c: (x, (y + step) % SIDE, z, c))


def along_ring(step, first_along_x):
    def move(x, y, z, c):
        if (c == 0) == first_along_x:
            return ((x + step) % SIDE, y, z, c)
        return (x, y, (z + step) % SIDE, c)

    return permutation(move)


CORE_SWAP = permutation(lambda x, y, z, c: (x, y, z, 1 - c))


def send(array, pairs):
    return lax.ppermute(array, AXES, pairs)


def gather(array, ring):
    return [array] + [send(array, ring(step)) for step in (1, -1, 2)]


def place():
    index = lax.axis_index("dp")
    return index >> 3, (index >> 1) & 3, index & 1


def project_kernel(*refs):
    x_refs, g_refs = refs[0:4], refs[4:8]
    key_hbm, value_hbm = refs[8:10]
    mine_ref, away_ref = refs[10:12]
    normed, weights, sems = refs[12:]
    rows = x_refs[0].shape[0]
    width = x_refs[0].shape[1]
    y = lax.axis_index("mp")
    core = place()[2]
    copies = []
    for slot in range(4):
        first = pl.multiple_of(((y + OFFSETS[slot]) & 3) * width, width)
        for which, hbm in enumerate((key_hbm, value_hbm)):
            copy = pltpu.make_async_copy(
                hbm.at[pl.ds(first, width), :], weights.at[which, slot], sems.at[which, slot]
            )
            copy.start()
            copies.append(copy)
    total = jnp.zeros((rows, 1), F32)
    for x_ref in x_refs:
        floats = x_ref[...].astype(F32)
        total += jnp.sum(floats * floats, axis=-1, keepdims=True)
    scale = lax.rsqrt(total * (1.0 / (4 * width)) + 1e-06)
    for slot in range(4):
        floats = x_refs[slot][...].astype(F32)
        normed[slot] = (floats * scale * g_refs[slot][...].astype(F32)).astype(BF16)
    for copy in copies:
        copy.wait()
    for half, out_ref in enumerate((mine_ref, away_ref)):
        first = pl.multiple_of((core ^ half) * HALF, HALF)
        for which in range(2):
            product = jnp.zeros((rows, HALF), F32)
            for slot in range(4):
                product += jnp.dot(
                    normed[slot],
                    weights[which, slot, :, pl.ds(first, HALF)],
                    preferred_element_type=F32,
                )
            for pair in range(PAIRS):
                for block in range(rows // BLOCK):
                    part = product[
                        block * BLOCK : (block + 1) * BLOCK, pair * TILE : (pair + 1) * TILE
                    ]
                    if which == 1:
                        part = part.T
                    out_ref[block, which, pair] = part.astype(BF16)


def project(states, gains, key_weight, value_weight):
    rows, width = states[0].shape
    blocks = rows // BLOCK
    shape = jax.ShapeDtypeStruct((blocks, 2, PAIRS, TILE, BLOCK), BF16)
    vmem = pl.BlockSpec(memory_space=pltpu.VMEM)
    hbm = pl.BlockSpec(memory_space=pl.ANY)
    return pl.pallas_call(
        project_kernel,
        out_shape=(shape, shape),
        in_specs=[vmem] * 8 + [hbm] * 2,
        out_specs=(vmem, vmem),
        scratch_shapes=[
            pltpu.VMEM((4, rows, width), BF16),
            pltpu.VMEM((2, 4, width, 2 * HALF), BF16),
            pltpu.SemaphoreType.DMA((2, 4)),
        ],
        compiler_params=pltpu.CompilerParams(vmem_limit_bytes=40 * 2**20),
        cost_estimate=pl.CostEstimate(
            flops=2 * rows * 4 * width * 4 * HALF, bytes_accessed=18 * 2**20, transcendentals=0
        ),
        name="project",
    )(*states, *gains, key_weight, value_weight)


def attend_kernel(*refs):
    wanted = refs[0]
    q_hbm, kv_hbm, out_hbm = refs[1:5], refs[5:9], refs[9:13]
    qbuf, kvbuf, masked, scores, sums, outbuf, chosen, in_sems, out_sems = refs[13:]
    x, z, core = place()
    copies = []
    for slot in range(4):
        copy = pltpu.make_async_copy(
            q_hbm[slot], qbuf.at[pl.ds(2 * slot, 2)], in_sems.at[0, slot]
        )
        copy.start()
        copies.append(copy)
        copy = pltpu.make_async_copy(
            kv_hbm[slot], kvbuf.at[pl.ds(2 * slot, 2)], in_sems.at[1, slot]
        )
        copy.start()
        copies.append(copy)
    for copy in copies:
        copy.wait()

    def dp_index(along_x, offset, swapped):
        ex = jnp.where(along_x, (x + offset) & 3, x)
        ez = jnp.where(along_x, z, (z + offset) & 3)
        return (ex * 4 + ez) * 2 + (core ^ swapped)

    lane_half = lax.broadcasted_iota(jnp.int32, (QTOK, TILE), 1) // HD
    row = lax.broadcasted_iota(jnp.int32, (16, 2 * BLOCK), 0) // 8
    col = lax.broadcasted_iota(jnp.int32, (16, 2 * BLOCK), 1) // BLOCK
    ones = jnp.where(row == col, 1.0, 0.0).astype(BF16)
    empty = jnp.zeros((HD, BLOCK), BF16)

    def question(index, carry):
        slot = index >> 1
        offset = jnp.where(slot == 0, 0, jnp.where(slot == 1, 3, jnp.where(slot == 2, 1, 2)))
        q_index = dp_index(core == 1, offset, index & 1)
        count = jnp.int32(0)
        for t in range(4):
            for swapped in range(2):
                local = wanted[q_index, dp_index(core == 0, OFFSETS[t], swapped)]
                chosen[count] = (t * 2 + swapped) * 2 + jnp.maximum(local, 0)
                count = count + jnp.where(local >= 0, 1, 0)
        for pair in range(PAIRS):
            part = qbuf[index, :, pair * TILE : (pair + 1) * TILE]
            for head in range(2):
                masked[pair, head] = jnp.where(lane_half == head, part, jnp.zeros_like(part))

        def score(step, tops):
            place_of = chosen[step]
            out = []
            for pair in range(PAIRS):
                keys = kvbuf[place_of >> 1, place_of & 1, 0, pair]
                for head in range(2):
                    s = lax.dot_general(
                        keys,
                        masked[pair, head],
                        (((1,), (1,)), ((), ())),
                        preferred_element_type=F32,
                    )
                    scores[step, pair, head] = s
                    top = jnp.max(s.reshape(BLOCK // 8, 8, QTOK), axis=0)
                    out.append(jnp.maximum(tops[2 * pair + head], top))
            return tuple(out)

        low = jnp.full((8, QTOK), -1e30, F32)
        tops = lax.fori_loop(0, count, score, (low,) * (2 * PAIRS))
        tops = [jnp.max(top, axis=0, keepdims=True) for top in tops]
        sums[...] = jnp.zeros_like(sums)

        def weigh(step, carry):
            place_of = chosen[step]
            for pair in range(PAIRS):
                probs = [
                    jnp.exp(scores[step, pair, head] - tops[2 * pair + head]).astype(BF16)
                    for head in range(2)
                ]
                values = kvbuf[place_of >> 1, place_of & 1, 1, pair]
                left = jnp.concatenate(
                    [
                        jnp.concatenate([values[:HD], empty], axis=1),
                        jnp.concatenate([empty, values[HD:]], axis=1),
                        ones,
                    ],
                    axis=0,
                )
                sums[pair] += jnp.dot(
                    left, jnp.concatenate(probs, axis=0), preferred_element_type=F32
                )
            return carry

        lax.fori_loop(0, count, weigh, 0)
        stats = []
        for pair in range(PAIRS):
            for head in range(2):
                total = sums[pair, TILE + 8 * head : TILE + 8 * head + 1, :]
                some = total > 0.0
                part = sums[pair, head * HD : (head + 1) * HD, :]
                part = part * (1.0 / jnp.where(some, total, 1.0))
                first = pair * TILE + head * HD
                outbuf[index, first : first + HD, :] = part.astype(BF16)
                top = tops[2 * pair + head]
                stats.append(jnp.where(some, top + jnp.log(jnp.where(some, total, 1.0)), -1e30))
        rest = jnp.concatenate(stats, axis=0)
        parts = []
        for _ in range(3):
            part = rest.astype(BF16).astype(F32)
            parts.append(part)
            rest = rest - part
        parts.append(jnp.zeros_like(rest))
        outbuf[index, HALF : HALF + STAT, :] = jnp.concatenate(parts, axis=0).astype(BF16)
        return carry

    lax.fori_loop(0, 8, question, 0)
    copies = []
    for slot in range(4):
        copy = pltpu.make_async_copy(
            outbuf.at[pl.ds(2 * slot, 2)], out_hbm[slot], out_sems.at[slot]
        )
        copy.start()
        copies.append(copy)
    for copy in copies:
        copy.wait()


def attend(wanted, queries, blocks):
    hbm = pl.BlockSpec(memory_space=pl.ANY)
    shape = jax.ShapeDtypeStruct((2, HALF + STAT, QTOK), BF16)
    return pl.pallas_call(
        attend_kernel,
        out_shape=(shape,) * 4,
        in_specs=[pl.BlockSpec(memory_space=pltpu.SMEM)] + [hbm] * 8,
        out_specs=(hbm,) * 4,
        scratch_shapes=[
            pltpu.VMEM((8, QTOK, HALF), BF16),
            pltpu.VMEM((8, 2, 2, PAIRS, TILE, BLOCK), BF16),
            pltpu.VMEM((PAIRS, 2, QTOK, TILE), BF16),
            pltpu.VMEM((8, PAIRS, 2, BLOCK, QTOK), F32),
            pltpu.VMEM((PAIRS, TILE + 16, QTOK), F32),
            pltpu.VMEM((8, HALF + STAT, QTOK), BF16),
            pltpu.SMEM((16,), jnp.int32),
            pltpu.SemaphoreType.DMA((2, 4)),
            pltpu.SemaphoreType.DMA((4,)),
        ],
        compiler_params=pltpu.CompilerParams(vmem_limit_bytes=40 * 2**20),
        name="attend",
    )(wanted, *queries, *blocks)


def merged(refs, which):
    stats = []
    for ref in refs:
        stat = ref[which, HALF : HALF + STAT, :].astype(F32)
        stats.append(stat[0:8] + stat[8:16] + stat[16:24])
    top = functools.reduce(jnp.maximum, stats)
    weights = [jnp.exp(stat - top) for stat in stats]
    inverse = 1.0 / sum(weights)
    weights = [weight * inverse for weight in weights]
    heads = []
    for head in range(2 * PAIRS):
        heads.append(
            sum(
                ref[which, head * HD : (head + 1) * HD, :].astype(F32) * weight[head : head + 1]
                for ref, weight in zip(refs, weights)
            )
        )
    return jnp.concatenate(heads, axis=0)


def merge_away_kernel(a, b, c, d, out_ref):
    out_ref[...] = merged((a, b, c, d), 1).T.astype(BF16)


def merge_home_kernel(a, b, c, d, other_ref, out_ref):
    core = place()[2]
    mine = pl.multiple_of(core * HALF, HALF)
    away = pl.multiple_of((1 - core) * HALF, HALF)
    out_ref[:, pl.ds(mine, HALF)] = merged((a, b, c, d), 0).T.astype(BF16)
    out_ref[:, pl.ds(away, HALF)] = other_ref[...]


def merge(partials):
    vmem = pl.BlockSpec(memory_space=pltpu.VMEM)
    away = pl.pallas_call(
        merge_away_kernel,
        out_shape=jax.ShapeDtypeStruct((QTOK, HALF), BF16),
        in_specs=[vmem] * 4,
        out_specs=vmem,
        name="merge_away",
    )(*partials)
    other = send(away, CORE_SWAP)
    return pl.pallas_call(
        merge_home_kernel,
        out_shape=jax.ShapeDtypeStruct((QTOK, 2 * HALF), BF16),
        in_specs=[vmem] * 5,
        out_specs=vmem,
        name="merge_home",
    )(*partials, other)


def both_cores(mine, away):
    return jnp.concatenate([mine, send(away, CORE_SWAP)], axis=0)


def local(block_states, norm_gain, key_weight, value_weight, queries, wanted):
    core = place()[2]
    states = gather(block_states.reshape(2 * BLOCK, -1), along_y)
    gains = gather(norm_gain.reshape(1, -1), along_y)
    mine = lax.dynamic_slice_in_dim(queries, core * HALF, HALF, 1)
    away = lax.dynamic_slice_in_dim(queries, (1 - core) * HALF, HALF, 1)
    kv_ring = functools.partial(along_ring, first_along_x=True)
    q_ring = functools.partial(along_ring, first_along_x=False)
    slots_q = gather(both_cores(mine[None], away[None]), q_ring)
    mine, away = project(states, gains, key_weight, value_weight)
    slots_kv = gather(both_cores(mine[None], away[None]), kv_ring)
    partials = attend(wanted, slots_q, slots_kv)
    returned = [partials[0]] + [
        send(partial, q_ring(-step)) for partial, step in zip(partials[1:], (1, -1, 2))
    ]
    return merge(returned)


def solution(mesh):
    return jax.shard_map(
        local,
        mesh=mesh,
        in_specs=(P("dp", None, "mp"), P("mp"), P(None, "mp"), P(None, "mp"), P("dp", "mp"), P()),
        out_specs=P("dp", "mp"),
        check_vma=False,
    )
```

```python
import functools

import jax
import jax.numpy as jnp
from jax import lax
from jax.experimental import pallas as pl
from jax.experimental.pallas import tpu as pltpu
from jax.sharding import PartitionSpec as P

AXES = ("dp", "mp")
SIDE = 4
HD = 64
BLOCK = 128
ROWS = 2 * BLOCK
HALF = 512
PAIRS = 4
PART = 2
TILE = 128
QTOK = 256
STAT = 32
SUMS = TILE + 16
LOW = -1e30
OFFSETS = (0, 3, 1, 2)
F32, BF16 = jnp.float32, jnp.bfloat16
MIB = 2**20


def device_id(x, y, z, c):
    return ((x * SIDE + z) * 2 + c) * SIDE + y


def permutation(move):
    pairs = []
    for x in range(SIDE):
        for z in range(SIDE):
            for c in range(2):
                for y in range(SIDE):
                    pairs.append((device_id(x, y, z, c), device_id(*move(x, y, z, c))))
    return pairs


def along_y(step):
    return permutation(lambda x, y, z, c: (x, (y + step) % SIDE, z, c))


def along_ring(step, first_along_x, cross=0):
    def move(x, y, z, c):
        if (c == 0) == first_along_x:
            return ((x + step) % SIDE, y, z, c ^ cross)
        return (x, y, (z + step) % SIDE, c ^ cross)

    return permutation(move)


CORE_SWAP = permutation(lambda x, y, z, c: (x, y, z, 1 - c))


def send(array, pairs):
    return lax.ppermute(array, AXES, pairs)


def gather(array, ring):
    far = send(array, ring(2))
    return [array, send(array, ring(1)), send(array, ring(-1)), far]


def place():
    index = lax.axis_index("dp")
    return index >> 3, (index >> 1) & 3, index & 1


def vmem():
    return pl.BlockSpec(memory_space=pltpu.VMEM)


def anywhere():
    return pl.BlockSpec(memory_space=pl.ANY)


def preload_kernel(key_hbm, value_hbm, key_out, value_out, sems):
    copies = [
        pltpu.make_async_copy(key_hbm, key_out, sems.at[0]),
        pltpu.make_async_copy(value_hbm, value_out, sems.at[1]),
    ]
    for copy in copies:
        copy.start()
    for copy in copies:
        copy.wait()


def preload(key_weight, value_weight):
    return pl.pallas_call(
        preload_kernel,
        out_shape=(pltpu.VMEM(key_weight.shape, BF16),) * 2,
        in_specs=[anywhere()] * 2,
        out_specs=(vmem(),) * 2,
        scratch_shapes=[pltpu.SemaphoreType.DMA((2,))],
        compiler_params=pltpu.CompilerParams(vmem_limit_bytes=20 * MIB),
        cost_estimate=pl.CostEstimate(flops=0, bytes_accessed=1024, transcendentals=0),
        name="preload",
    )(key_weight, value_weight)


def normalise(x_refs, gain_refs, normed):
    width = x_refs[0].shape[1]
    for block in range(2):
        rows = pl.ds(block * BLOCK, BLOCK)
        parts = [x_ref[rows, :] for x_ref in x_refs[:3]] + [x_refs[3 + block][...]]
        total = jnp.zeros((BLOCK, 1), F32)
        for part in parts:
            floats = part.astype(F32)
            total += jnp.sum(floats * floats, axis=-1, keepdims=True)
        scale = lax.rsqrt(total * (1.0 / (4 * width)) + 1e-06)
        for slot, part in enumerate(parts):
            gain = gain_refs[slot][...].reshape(1, width).astype(F32)
            normed[slot, rows, :] = (part.astype(F32) * scale * gain).astype(BF16)


def project_kernel(part, *refs):
    refs = list(refs)
    if part == 0:
        x_refs = [refs.pop(0) for _ in range(5)]
        gain_refs = [refs.pop(0) for _ in range(4)]
    else:
        normed = refs.pop(0)
    weight_refs = [refs.pop(0) for _ in range(2)]
    mine_ref, away_ref = refs[0:2]
    if part == 0:
        normed = refs[2]
        normalise(x_refs, gain_refs, normed)
    width = normed.shape[2]
    columns = PART * TILE
    y = lax.axis_index("mp")
    core = place()[2]
    for half, out_ref in enumerate((away_ref, mine_ref)):
        column = pl.multiple_of((core ^ (1 - half)) * HALF + part * columns, columns)
        for which in range(2):
            product = jnp.zeros((ROWS, columns), F32)
            for slot in range(4):
                row = pl.multiple_of(((y + OFFSETS[slot]) & 3) * width, width)
                product += jnp.dot(
                    normed[slot],
                    weight_refs[which][pl.ds(row, width), pl.ds(column, columns)],
                    preferred_element_type=F32,
                )
            for block in range(2):
                for pair in range(PART):
                    tile = product[
                        block * BLOCK : (block + 1) * BLOCK, pair * TILE : (pair + 1) * TILE
                    ]
                    if which == 1:
                        tile = tile.T
                    out_ref[block, which, pair] = tile.astype(BF16)


def project(part, inputs, key_weight, value_weight):
    shapes = [jax.ShapeDtypeStruct((2, 2, PART, TILE, BLOCK), BF16)] * 2
    if part == 0:
        shapes.append(jax.ShapeDtypeStruct((4, ROWS, inputs[0].shape[1]), BF16))
    return pl.pallas_call(
        functools.partial(project_kernel, part),
        out_shape=tuple(shapes),
        in_specs=[vmem()] * (len(inputs) + 2),
        out_specs=(vmem(),) * len(shapes),
        compiler_params=pltpu.CompilerParams(vmem_limit_bytes=28 * MIB),
        cost_estimate=pl.CostEstimate(flops=0, bytes_accessed=1024, transcendentals=0),
        name="project",
    )(*inputs, key_weight, value_weight)


def spread(top):
    def rows(pair):
        a = top[2 * pair : 2 * pair + 1]
        b = top[2 * pair + 1 : 2 * pair + 2]
        return jnp.concatenate(
            [
                jnp.broadcast_to(a, (HD, QTOK)),
                jnp.broadcast_to(b, (HD, QTOK)),
                jnp.broadcast_to(a, (8, QTOK)),
                jnp.broadcast_to(b, (8, QTOK)),
            ],
            axis=0,
        )

    return rows


def attend_kernel(part, slots, *refs):
    refs = list(refs)
    take = lambda n: [refs.pop(0) for _ in range(n)]
    wanted = refs.pop(0)
    q_hbm, kv_hbm = take(len(slots)), take(4)
    if part:
        early_out, early_stats = take(2)
        outs = take(2 * len(slots))
    else:
        early_out, early_stats = take(2)
    qbuf, kvbuf, masked, scores, run_sums, run_tops, chosen, in_sems = take(8)
    x, z, core = place()
    columns = pl.ds(part * PART * TILE, PART * TILE)
    copies = []
    for number in range(len(slots)):
        copies.append(
            pltpu.make_async_copy(
                q_hbm[number].at[:, :, columns],
                qbuf.at[pl.ds(2 * number, 2)],
                in_sems.at[4 + number],
            )
        )
    for t in range(4):
        copies.append(
            pltpu.make_async_copy(kv_hbm[t], kvbuf.at[pl.ds(2 * t, 2)], in_sems.at[t])
        )
    for copy in copies:
        copy.start()
    for copy in copies:
        copy.wait()

    def dp_index(along_x, offset, swapped):
        ex = jnp.where(along_x, (x + offset) & 3, x)
        ez = jnp.where(along_x, z, (z + offset) & 3)
        return (ex * 4 + ez) * 2 + (core ^ swapped)

    lane_half = lax.broadcasted_iota(jnp.int32, (QTOK, TILE), 1) // HD
    row = lax.broadcasted_iota(jnp.int32, (16, 2 * BLOCK), 0) // 8
    col = lax.broadcasted_iota(jnp.int32, (16, 2 * BLOCK), 1) // BLOCK
    ones = jnp.where(row == col, 1.0, 0.0).astype(BF16)
    empty = jnp.zeros((HD, BLOCK), BF16)

    def question(index, carry):
        number = index >> 1
        offset, offset_slot = jnp.int32(OFFSETS[slots[0]]), jnp.int32(slots[0])
        for other in range(1, len(slots)):
            offset = jnp.where(number == other, OFFSETS[slots[other]], offset)
            offset_slot = jnp.where(number == other, slots[other], offset_slot)
        q_index = dp_index(core == 1, offset, index & 1)
        count = jnp.int32(0)
        for t in range(4):
            for swapped in range(2):
                local = wanted[q_index, dp_index(core == 0, OFFSETS[t], swapped)]
                chosen[count] = (t * 2 + swapped) * 2 + jnp.maximum(local, 0)
                count = count + jnp.where(local >= 0, 1, 0)
        for pair in range(PART):
            query = qbuf[index, :, pair * TILE : (pair + 1) * TILE]
            for head in range(2):
                masked[pair, head] = jnp.where(lane_half == head, query, jnp.zeros_like(query))
        run_sums[...] = jnp.zeros((PART, SUMS, QTOK), F32)
        run_tops[...] = jnp.full((8, QTOK), LOW, F32)
        chosen[count] = chosen[jnp.maximum(count - 1, 0)]

        def weigh(size):
            places = [chosen[step] for step in range(size)]
            live = (count == size).astype(BF16)
            rows = []
            for pair in range(PART):
                keys = [kvbuf[where >> 1, where & 1, 0, pair] for where in places]
                keys = jnp.concatenate(keys, axis=0)
                for head in range(2):
                    s = lax.dot_general(
                        keys,
                        masked[pair, head],
                        (((1,), (1,)), ((), ())),
                        preferred_element_type=F32,
                    )
                    rows.append(jnp.max(s, axis=0, keepdims=True))
                    scores[:size, pair, head] = s.reshape(size, BLOCK, QTOK)
            run_tops[...] = jnp.concatenate(rows + rows, axis=0)
            for pair in range(PART):
                left, probs = [], []
                for step, where in enumerate(places):
                    for head in range(2):
                        shifted = scores[step, pair, head] - rows[2 * pair + head]
                        probs.append(jnp.exp(shifted).astype(BF16))
                    values, unit = kvbuf[where >> 1, where & 1, 1, pair], ones
                    if step == size - 1:
                        values, unit = values * live, unit * live
                    left.append(
                        jnp.concatenate(
                            [
                                jnp.concatenate([values[:HD], empty], axis=1),
                                jnp.concatenate([empty, values[HD:]], axis=1),
                                unit,
                            ],
                            axis=0,
                        )
                    )
                run_sums[pair] = jnp.dot(
                    jnp.concatenate(left, axis=1),
                    jnp.concatenate(probs, axis=0),
                    preferred_element_type=F32,
                )

        for size in (2, 4, 6, 8):

            @pl.when((count + 1) >> 1 == size // 2)
            def _(size=size):
                weigh(size)

        tops = run_tops[...]
        totals = []
        finished = []
        for pair in range(PART):
            done = run_sums[pair]
            finished.append(done)
            totals += [done[TILE : TILE + 1], done[TILE + 8 : TILE + 9]]
        total = jnp.concatenate(totals, axis=0)
        some = total > 0.0
        safe = jnp.where(some, total, 1.0)
        inverse = spread(1.0 / safe)
        pieces = [(done * inverse(pair))[:TILE].astype(BF16) for pair, done in enumerate(finished)]
        stat = jnp.where(some, tops[: 2 * PART] + jnp.log(safe), LOW)
        if part == 0:
            early_out[index] = jnp.concatenate(pieces, axis=0)
            early_stats[index] = jnp.concatenate([stat, stat], axis=0)
            return carry
        early = 2 * offset_slot + (index & 1)
        rest = jnp.concatenate([early_stats[early][: 2 * PART], stat], axis=0)
        pieces = [early_out[early]] + pieces
        stats = []
        for _ in range(3):
            rounded = rest.astype(BF16).astype(F32)
            stats.append(rounded)
            rest = rest - rounded
        stats.append(jnp.zeros_like(rest))
        pieces.append(jnp.concatenate(stats, axis=0).astype(BF16))
        message = jnp.concatenate(pieces, axis=0)
        for other in range(2 * len(slots)):

            @pl.when(index == other)
            def _(other=other):
                outs[other][...] = message

        return carry

    lax.fori_loop(0, 2 * len(slots), question, 0)


def attend(part, wanted, queries, blocks, slots, early=()):
    count = 2 * len(slots)
    if part:
        out_shape = (jax.ShapeDtypeStruct((HALF + STAT, QTOK), BF16),) * count
    else:
        out_shape = (
            jax.ShapeDtypeStruct((count, PART * TILE, QTOK), BF16),
            jax.ShapeDtypeStruct((count, 8, QTOK), F32),
        )
    return pl.pallas_call(
        functools.partial(attend_kernel, part, slots),
        out_shape=out_shape,
        in_specs=[pl.BlockSpec(memory_space=pltpu.SMEM)]
        + [anywhere()] * (len(slots) + 4)
        + [vmem()] * len(early),
        out_specs=(vmem(),) * len(out_shape),
        scratch_shapes=[
            pltpu.VMEM((count, QTOK, PART * TILE), BF16),
            pltpu.VMEM((8, 2, 2, PART, TILE, BLOCK), BF16),
            pltpu.VMEM((PART, 2, QTOK, TILE), BF16),
            pltpu.VMEM((8, PART, 2, BLOCK, QTOK), F32),
            pltpu.VMEM((PART, SUMS, QTOK), F32),
            pltpu.VMEM((8, QTOK), F32),
            pltpu.SMEM((16,), jnp.int32),
            pltpu.SemaphoreType.DMA((4 + len(slots),)),
        ],
        compiler_params=pltpu.CompilerParams(vmem_limit_bytes=24 * MIB),
        cost_estimate=pl.CostEstimate(
            flops=count * 10**9, bytes_accessed=8 * MIB, transcendentals=0
        ),
        name="attend",
    )(wanted, *[queries[slot] for slot in slots], *blocks, *early)


def merged(refs):
    stats = []
    for ref in refs:
        stat = ref[HALF : HALF + STAT, :].astype(F32)
        stats.append(stat[0:8] + stat[8:16] + stat[16:24])
    top = functools.reduce(jnp.maximum, stats)
    weights = [jnp.exp(stat - top) for stat in stats]
    inverse = 1.0 / sum(weights)
    weights = [weight * inverse for weight in weights]
    heads = []
    for head in range(2 * PAIRS):
        heads.append(
            sum(
                ref[head * HD : (head + 1) * HD, :].astype(F32) * weight[head : head + 1]
                for ref, weight in zip(refs, weights)
            ).astype(BF16)
        )
    row = lax.broadcasted_iota(jnp.int32, (QTOK, QTOK), 0)
    col = lax.broadcasted_iota(jnp.int32, (QTOK, QTOK), 1)
    unit = jnp.where(row == col, 1.0, 0.0).astype(BF16)
    return lax.dot_general(
        unit,
        jnp.concatenate(heads, axis=0),
        (((1,), (1,)), ((), ())),
        preferred_element_type=F32,
    )


def merge_kernel(*refs):
    out_ref = refs[8]
    core = place()[2]
    for half in range(2):
        column = pl.multiple_of((core ^ half) * HALF, HALF)
        out_ref[:, pl.ds(column, HALF)] = merged(refs[4 * half : 4 * half + 4]).astype(BF16)


def merge(mine, away):
    return pl.pallas_call(
        merge_kernel,
        out_shape=jax.ShapeDtypeStruct((QTOK, 2 * HALF), BF16),
        in_specs=[vmem()] * 8,
        out_specs=vmem(),
        compiler_params=pltpu.CompilerParams(vmem_limit_bytes=16 * MIB),
        name="merge",
    )(*mine, *away)


def both_cores(mine, away):
    return jnp.concatenate([mine[None], send(away, CORE_SWAP)[None]], axis=0)


def local(block_states, norm_gain, key_weight, value_weight, queries, wanted):
    kv_ring = functools.partial(along_ring, first_along_x=True)
    q_ring = functools.partial(along_ring, first_along_x=False)
    core = place()[2]
    own = block_states.reshape(ROWS, block_states.shape[2])
    left, right = send(own, along_y(1)), send(own, along_y(-1))
    gains = gather(norm_gain, along_y)
    mine = lax.dynamic_slice_in_dim(queries, core * HALF, HALF, 1)
    away = lax.dynamic_slice_in_dim(queries, (1 - core) * HALF, HALF, 1)
    slots_q = gather(both_cores(mine, away), q_ring)
    key_weight, value_weight = preload(key_weight, value_weight)
    far = [send(left[:BLOCK], along_y(1)), send(right[BLOCK:], along_y(-1))]
    *slots_q, far[1] = lax.optimization_barrier((*slots_q, far[1]))
    inputs = [own, left, right, *far, *gains]
    *ready, normed = project(0, inputs, key_weight, value_weight)
    kv = gather(both_cores(*ready), kv_ring)
    kv_late = gather(both_cores(*project(1, [normed], key_weight, value_weight)), kv_ring)
    early = attend(0, wanted, slots_q, kv, (0, 1, 2, 3))
    mine, away = [], []
    for slots in ((3, 1), (2,), (0,)):
        outs = attend(1, wanted, slots_q, kv_late, slots, early)
        for number, slot in enumerate(slots):
            same, cross = outs[2 * number : 2 * number + 2]
            step = OFFSETS[slot]
            mine.append(send(same, q_ring(step)) if slot else same)
            away.append(send(cross, q_ring(step, cross=1)))
    return merge(mine, away)


def solution(mesh):
    return jax.shard_map(
        local,
        mesh=mesh,
        in_specs=(P("dp", None, "mp"), P("mp"), P(None, "mp"), P(None, "mp"), P("dp", "mp"), P()),
        out_specs=P("dp", "mp"),
        check_vma=False,
    )
```

```python
import functools

import jax
import jax.numpy as jnp
from jax import lax
from jax.experimental import pallas as pl
from jax.experimental.pallas import tpu as pltpu
from jax.sharding import PartitionSpec as P

AXES = ("dp", "mp")
SIDE = 4
HD = 64
BLOCK = 128
ROWS = 2 * BLOCK
HALF = 512
PAIRS = 4
PART = 2
TILE = 128
QTOK = 256
STAT = 32
SUMS = TILE + 16
LOW = -1e30
OFFSETS = (0, 3, 1, 2)
F32, BF16 = jnp.float32, jnp.bfloat16
MIB = 2**20


def device_id(x, y, z, c):
    return ((x * SIDE + z) * 2 + c) * SIDE + y


def permutation(move):
    pairs = []
    for x in range(SIDE):
        for z in range(SIDE):
            for c in range(2):
                for y in range(SIDE):
                    pairs.append((device_id(x, y, z, c), device_id(*move(x, y, z, c))))
    return pairs


def along_y(step):
    return permutation(lambda x, y, z, c: (x, (y + step) % SIDE, z, c))


def along_ring(step, first_along_x, cross=0):
    def move(x, y, z, c):
        if (c == 0) == first_along_x:
            return ((x + step) % SIDE, y, z, c ^ cross)
        return (x, y, (z + step) % SIDE, c ^ cross)

    return permutation(move)


CORE_SWAP = permutation(lambda x, y, z, c: (x, y, z, 1 - c))


def send(array, pairs):
    return lax.ppermute(array, AXES, pairs)


def gather(array, ring):
    far = send(array, ring(2))
    return [array, send(array, ring(1)), send(array, ring(-1)), far]


def place():
    index = lax.axis_index("dp")
    return index >> 3, (index >> 1) & 3, index & 1


def vmem():
    return pl.BlockSpec(memory_space=pltpu.VMEM)


def anywhere():
    return pl.BlockSpec(memory_space=pl.ANY)


def preload_kernel(key_hbm, value_hbm, key_out, value_out, sems):
    copies = [
        pltpu.make_async_copy(key_hbm, key_out, sems.at[0]),
        pltpu.make_async_copy(value_hbm, value_out, sems.at[1]),
    ]
    for copy in copies:
        copy.start()
    for copy in copies:
        copy.wait()


def preload(key_weight, value_weight):
    return pl.pallas_call(
        preload_kernel,
        out_shape=(pltpu.VMEM(key_weight.shape, BF16),) * 2,
        in_specs=[anywhere()] * 2,
        out_specs=(vmem(),) * 2,
        scratch_shapes=[pltpu.SemaphoreType.DMA((2,))],
        compiler_params=pltpu.CompilerParams(vmem_limit_bytes=2 * MIB),
        cost_estimate=pl.CostEstimate(flops=0, bytes_accessed=1024, transcendentals=0),
        name="preload",
    )(key_weight, value_weight)


def normalise(x_refs, gain_refs, normed):
    width = x_refs[0].shape[1]
    gains = [gain_refs[0][...].reshape(1, width).astype(F32)]
    gains += [far[BLOCK:, :].astype(F32)[0:1] for far in x_refs[3:]]
    gains += [gain_refs[1][...].reshape(1, width).astype(F32)]
    for block in range(2):
        rows = pl.ds(block * BLOCK, BLOCK)
        parts = [x_ref[rows, :] for x_ref in x_refs[:3]] + [x_refs[3 + block][:BLOCK, :]]
        total = jnp.zeros((BLOCK, 1), F32)
        for part in parts:
            floats = part.astype(F32)
            total += jnp.sum(floats * floats, axis=-1, keepdims=True)
        scale = lax.rsqrt(total * (1.0 / (4 * width)) + 1e-06)
        for slot, part in enumerate(parts):
            normed[slot, rows, :] = (part.astype(F32) * scale * gains[slot]).astype(BF16)


def project_kernel(part, *refs):
    refs = list(refs)
    if part == 0:
        x_refs = [refs.pop(0) for _ in range(5)]
        gain_refs = [refs.pop(0) for _ in range(2)]
    else:
        normed = refs.pop(0)
    weight_refs = [refs.pop(0) for _ in range(2)]
    mine_ref, away_ref = refs[0:2]
    if part == 0:
        normed = refs[2]
        normalise(x_refs, gain_refs, normed)
    width = normed.shape[2]
    columns = PART * TILE
    y = lax.axis_index("mp")
    core = place()[2]
    for half, out_ref in enumerate((away_ref, mine_ref)):
        column = pl.multiple_of((core ^ (1 - half)) * HALF + part * columns, columns)
        for which in range(2):
            product = jnp.zeros((ROWS, columns), F32)
            for slot in range(4):
                row = pl.multiple_of(((y + OFFSETS[slot]) & 3) * width, width)
                product += jnp.dot(
                    normed[slot],
                    weight_refs[which][pl.ds(row, width), pl.ds(column, columns)],
                    preferred_element_type=F32,
                )
            for block in range(2):
                for pair in range(PART):
                    tile = product[
                        block * BLOCK : (block + 1) * BLOCK, pair * TILE : (pair + 1) * TILE
                    ]
                    if which == 1:
                        tile = tile.T
                    out_ref[block, which, pair] = tile.astype(BF16)


def project(part, inputs, key_weight, value_weight):
    shapes = [jax.ShapeDtypeStruct((2, 2, PART, TILE, BLOCK), BF16)] * 2
    if part == 0:
        shapes.append(jax.ShapeDtypeStruct((4, ROWS, inputs[0].shape[1]), BF16))
    return pl.pallas_call(
        functools.partial(project_kernel, part),
        out_shape=tuple(shapes),
        in_specs=[vmem()] * (len(inputs) + 2),
        out_specs=(vmem(),) * len(shapes),
        compiler_params=pltpu.CompilerParams(vmem_limit_bytes=12 * MIB),
        cost_estimate=pl.CostEstimate(flops=0, bytes_accessed=1024, transcendentals=0),
        name="project",
    )(*inputs, key_weight, value_weight)


def spread(top):
    def rows(pair):
        a = top[2 * pair : 2 * pair + 1]
        b = top[2 * pair + 1 : 2 * pair + 2]
        return jnp.concatenate(
            [
                jnp.broadcast_to(a, (HD, QTOK)),
                jnp.broadcast_to(b, (HD, QTOK)),
                jnp.broadcast_to(a, (8, QTOK)),
                jnp.broadcast_to(b, (8, QTOK)),
            ],
            axis=0,
        )

    return rows


def attend_kernel(part, slots, *refs):
    refs = list(refs)
    take = lambda n: [refs.pop(0) for _ in range(n)]
    wanted = refs.pop(0)
    q_hbm, kv_hbm = take(len(slots)), take(4)
    if part:
        early_out, early_stats = take(2)
        outs = take(2 * len(slots))
    else:
        early_out, early_stats = take(2)
    qbuf, kvbuf, masked, scores, run_sums, run_tops, chosen, in_sems = take(8)
    x, z, core = place()
    columns = pl.ds(part * PART * TILE, PART * TILE)
    copies = []
    for number in range(len(slots)):
        copies.append(
            pltpu.make_async_copy(
                q_hbm[number].at[:, :, columns],
                qbuf.at[pl.ds(2 * number, 2)],
                in_sems.at[4 + number],
            )
        )
    for t in range(4):
        copies.append(
            pltpu.make_async_copy(kv_hbm[t], kvbuf.at[pl.ds(2 * t, 2)], in_sems.at[t])
        )
    for copy in copies:
        copy.start()
    for copy in copies:
        copy.wait()

    def dp_index(along_x, offset, swapped):
        ex = jnp.where(along_x, (x + offset) & 3, x)
        ez = jnp.where(along_x, z, (z + offset) & 3)
        return (ex * 4 + ez) * 2 + (core ^ swapped)

    lane_half = lax.broadcasted_iota(jnp.int32, (QTOK, TILE), 1) // HD
    row = lax.broadcasted_iota(jnp.int32, (16, 2 * BLOCK), 0) // 8
    col = lax.broadcasted_iota(jnp.int32, (16, 2 * BLOCK), 1) // BLOCK
    ones = jnp.where(row == col, 1.0, 0.0).astype(BF16)
    empty = jnp.zeros((HD, BLOCK), BF16)

    def question(index, carry):
        number = index >> 1
        offset, offset_slot = jnp.int32(OFFSETS[slots[0]]), jnp.int32(slots[0])
        for other in range(1, len(slots)):
            offset = jnp.where(number == other, OFFSETS[slots[other]], offset)
            offset_slot = jnp.where(number == other, slots[other], offset_slot)
        q_index = dp_index(core == 1, offset, index & 1)
        count = jnp.int32(0)
        for t in range(4):
            for swapped in range(2):
                local = wanted[q_index, dp_index(core == 0, OFFSETS[t], swapped)]
                chosen[count] = (t * 2 + swapped) * 2 + jnp.maximum(local, 0)
                count = count + jnp.where(local >= 0, 1, 0)
        for pair in range(PART):
            query = qbuf[index, :, pair * TILE : (pair + 1) * TILE]
            for head in range(2):
                masked[pair, head] = jnp.where(lane_half == head, query, jnp.zeros_like(query))
        run_sums[...] = jnp.zeros((PART, SUMS, QTOK), F32)
        run_tops[...] = jnp.full((8, QTOK), LOW, F32)
        chosen[count] = chosen[jnp.maximum(count - 1, 0)]

        def weigh(size):
            places = [chosen[step] for step in range(size)]
            live = (count == size).astype(BF16)
            rows = []
            for pair in range(PART):
                keys = [kvbuf[where >> 1, where & 1, 0, pair] for where in places]
                keys = jnp.concatenate(keys, axis=0)
                for head in range(2):
                    s = lax.dot_general(
                        keys,
                        masked[pair, head],
                        (((1,), (1,)), ((), ())),
                        preferred_element_type=F32,
                    )
                    rows.append(jnp.max(s, axis=0, keepdims=True))
                    scores[:size, pair, head] = s.reshape(size, BLOCK, QTOK)
            run_tops[...] = jnp.concatenate(rows + rows, axis=0)
            for pair in range(PART):
                left, probs = [], []
                for step, where in enumerate(places):
                    for head in range(2):
                        shifted = scores[step, pair, head] - rows[2 * pair + head]
                        probs.append(jnp.exp(shifted).astype(BF16))
                    values, unit = kvbuf[where >> 1, where & 1, 1, pair], ones
                    if step == size - 1:
                        values, unit = values * live, unit * live
                    left.append(
                        jnp.concatenate(
                            [
                                jnp.concatenate([values[:HD], empty], axis=1),
                                jnp.concatenate([empty, values[HD:]], axis=1),
                                unit,
                            ],
                            axis=0,
                        )
                    )
                run_sums[pair] = jnp.dot(
                    jnp.concatenate(left, axis=1),
                    jnp.concatenate(probs, axis=0),
                    preferred_element_type=F32,
                )

        for size in (2, 4, 6, 8):

            @pl.when((count + 1) >> 1 == size // 2)
            def _(size=size):
                weigh(size)

        tops = run_tops[...]
        totals = []
        finished = []
        for pair in range(PART):
            done = run_sums[pair]
            finished.append(done)
            totals += [done[TILE : TILE + 1], done[TILE + 8 : TILE + 9]]
        total = jnp.concatenate(totals, axis=0)
        some = total > 0.0
        safe = jnp.where(some, total, 1.0)
        inverse = spread(1.0 / safe)
        pieces = [(done * inverse(pair))[:TILE].astype(BF16) for pair, done in enumerate(finished)]
        stat = jnp.where(some, tops[: 2 * PART] + jnp.log(safe), LOW)
        if part == 0:
            early_out[index] = jnp.concatenate(pieces, axis=0)
            early_stats[index] = jnp.concatenate([stat, stat], axis=0)
            return carry
        early = 2 * offset_slot + (index & 1)
        rest = jnp.concatenate([early_stats[early][: 2 * PART], stat], axis=0)
        pieces = [early_out[early]] + pieces
        stats = []
        for _ in range(3):
            rounded = rest.astype(BF16).astype(F32)
            stats.append(rounded)
            rest = rest - rounded
        stats.append(jnp.zeros_like(rest))
        pieces.append(jnp.concatenate(stats, axis=0).astype(BF16))
        message = jnp.concatenate(pieces, axis=0)
        for other in range(2 * len(slots)):

            @pl.when(index == other)
            def _(other=other):
                outs[other][...] = message

        return carry

    lax.fori_loop(0, 2 * len(slots), question, 0)


def attend(part, wanted, queries, blocks, slots, early=()):
    count = 2 * len(slots)
    if part:
        out_shape = (jax.ShapeDtypeStruct((HALF + STAT, QTOK), BF16),) * count
    else:
        out_shape = (
            jax.ShapeDtypeStruct((count, PART * TILE, QTOK), BF16),
            jax.ShapeDtypeStruct((count, 8, QTOK), F32),
        )
    return pl.pallas_call(
        functools.partial(attend_kernel, part, slots),
        out_shape=out_shape,
        in_specs=[pl.BlockSpec(memory_space=pltpu.SMEM)]
        + [anywhere()] * (len(slots) + 4)
        + [vmem()] * len(early),
        out_specs=(vmem(),) * len(out_shape),
        scratch_shapes=[
            pltpu.VMEM((count, QTOK, PART * TILE), BF16),
            pltpu.VMEM((8, 2, 2, PART, TILE, BLOCK), BF16),
            pltpu.VMEM((PART, 2, QTOK, TILE), BF16),
            pltpu.VMEM((8, PART, 2, BLOCK, QTOK), F32),
            pltpu.VMEM((PART, SUMS, QTOK), F32),
            pltpu.VMEM((8, QTOK), F32),
            pltpu.SMEM((16,), jnp.int32),
            pltpu.SemaphoreType.DMA((4 + len(slots),)),
        ],
        compiler_params=pltpu.CompilerParams(vmem_limit_bytes=24 * MIB),
        cost_estimate=pl.CostEstimate(
            flops=count * 10**9, bytes_accessed=8 * MIB, transcendentals=0
        ),
        name="attend",
    )(wanted, *[queries[slot] for slot in slots], *blocks, *early)


def merged(refs):
    stats = []
    for ref in refs:
        stat = ref[HALF : HALF + STAT, :].astype(F32)
        stats.append(stat[0:8] + stat[8:16] + stat[16:24])
    top = functools.reduce(jnp.maximum, stats)
    weights = [jnp.exp(stat - top) for stat in stats]
    inverse = 1.0 / sum(weights)
    weights = [weight * inverse for weight in weights]
    heads = []
    for head in range(2 * PAIRS):
        heads.append(
            sum(
                ref[head * HD : (head + 1) * HD, :].astype(F32) * weight[head : head + 1]
                for ref, weight in zip(refs, weights)
            ).astype(BF16)
        )
    row = lax.broadcasted_iota(jnp.int32, (QTOK, QTOK), 0)
    col = lax.broadcasted_iota(jnp.int32, (QTOK, QTOK), 1)
    unit = jnp.where(row == col, 1.0, 0.0).astype(BF16)
    return lax.dot_general(
        unit,
        jnp.concatenate(heads, axis=0),
        (((1,), (1,)), ((), ())),
        preferred_element_type=F32,
    )


def merge_kernel(*refs):
    out_ref = refs[8]
    core = place()[2]
    for half in range(2):
        column = pl.multiple_of((core ^ half) * HALF, HALF)
        out_ref[:, pl.ds(column, HALF)] = merged(refs[4 * half : 4 * half + 4]).astype(BF16)


def merge(mine, away):
    return pl.pallas_call(
        merge_kernel,
        out_shape=jax.ShapeDtypeStruct((QTOK, 2 * HALF), BF16),
        in_specs=[vmem()] * 8,
        out_specs=vmem(),
        compiler_params=pltpu.CompilerParams(vmem_limit_bytes=16 * MIB),
        name="merge",
    )(*mine, *away)


def both_cores(mine, away):
    return jnp.concatenate([mine[None], send(away, CORE_SWAP)[None]], axis=0)


def local(block_states, norm_gain, key_weight, value_weight, queries, wanted):
    kv_ring = functools.partial(along_ring, first_along_x=True)
    q_ring = functools.partial(along_ring, first_along_x=False)
    core = place()[2]
    own = block_states.reshape(ROWS, block_states.shape[2])
    left, right = send(own, along_y(1)), send(own, along_y(-1))
    far_gain = send(norm_gain, along_y(2))
    other = send(queries, CORE_SWAP)
    halves = [lax.dynamic_slice_in_dim(each, core * HALF, HALF, 1)[None] for each in (queries, other)]
    q_pair = jnp.concatenate(halves, axis=0)
    q_far, q_right = send(q_pair, q_ring(2)), send(q_pair, q_ring(-1))
    gain_rows = jnp.broadcast_to(norm_gain[None], (16, norm_gain.shape[0]))
    key_weight, value_weight = preload(key_weight, value_weight)
    left, right, key_weight, value_weight = lax.optimization_barrier(
        (left, right, key_weight, value_weight)
    )
    far = [
        send(jnp.concatenate([left[:BLOCK], gain_rows], axis=0), along_y(1)),
        send(jnp.concatenate([right[BLOCK:], gain_rows], axis=0), along_y(-1)),
    ]
    q_left = send(lax.optimization_barrier((q_pair, left))[0], q_ring(1))
    q_far, q_right, far[0] = lax.optimization_barrier((q_far, q_right, far[0]))
    inputs = [own, left, right, *far, norm_gain, far_gain]
    *ready, normed = project(0, inputs, key_weight, value_weight)
    kv = gather(both_cores(*ready), kv_ring)
    normed, q_left = lax.optimization_barrier((normed, q_left))
    kv_late = gather(both_cores(*project(1, [normed], key_weight, value_weight)), kv_ring)
    slots_q = [q_pair, q_left, q_right, q_far]
    early = attend(0, wanted, slots_q, kv, (0, 1, 2, 3))
    mine, away = [], []
    for slots in ((3, 1), (2,), (0,)):
        outs = attend(1, wanted, slots_q, kv_late, slots, early)
        for number, slot in enumerate(slots):
            same, cross = outs[2 * number : 2 * number + 2]
            step = OFFSETS[slot]
            mine.append(send(same, q_ring(step)) if slot else same)
            away.append(send(cross, q_ring(step, cross=1)))
    return merge(mine, away)


def solution(mesh):
    return jax.shard_map(
        local,
        mesh=mesh,
        in_specs=(P("dp", None, "mp"), P("mp"), P(None, "mp"), P(None, "mp"), P("dp", "mp"), P()),
        out_specs=P("dp", "mp"),
        check_vma=False,
    )
```

```python
import functools

import jax
import jax.numpy as jnp
from jax import lax
from jax.experimental import pallas as pl
from jax.experimental.pallas import tpu as pltpu
from jax.sharding import PartitionSpec as P

AXES = ("dp", "mp")
SIDE = 4
HD = 64
BLOCK = 128
ROWS = 2 * BLOCK
HALF = 512
PAIRS = 4
PART = 2
TILE = 128
QTOK = 256
STAT = 32
SUMS = TILE + 16
LOW = -1e30
OFFSETS = (0, 3, 1, 2)
F32, BF16 = jnp.float32, jnp.bfloat16
MIB = 2**20


def device_id(x, y, z, c):
    return ((x * SIDE + z) * 2 + c) * SIDE + y


def permutation(move):
    pairs = []
    for x in range(SIDE):
        for z in range(SIDE):
            for c in range(2):
                for y in range(SIDE):
                    pairs.append((device_id(x, y, z, c), device_id(*move(x, y, z, c))))
    return pairs


def along_y(step):
    return permutation(lambda x, y, z, c: (x, (y + step) % SIDE, z, c))


def along_ring(step, first_along_x, cross=0):
    def move(x, y, z, c):
        if (c == 0) == first_along_x:
            return ((x + step) % SIDE, y, z, c ^ cross)
        return (x, y, (z + step) % SIDE, c ^ cross)

    return permutation(move)


CORE_SWAP = permutation(lambda x, y, z, c: (x, y, z, 1 - c))


def send(array, pairs):
    return lax.ppermute(array, AXES, pairs)


def gather(array, ring):
    far = send(array, ring(2))
    return [array, send(array, ring(1)), send(array, ring(-1)), far]


def place():
    index = lax.axis_index("dp")
    return index >> 3, (index >> 1) & 3, index & 1


def vmem():
    return pl.BlockSpec(memory_space=pltpu.VMEM)


def anywhere():
    return pl.BlockSpec(memory_space=pl.ANY)


def preload_kernel(key_hbm, value_hbm, key_out, value_out, sems):
    copies = [
        pltpu.make_async_copy(key_hbm, key_out, sems.at[0]),
        pltpu.make_async_copy(value_hbm, value_out, sems.at[1]),
    ]
    for copy in copies:
        copy.start()
    for copy in copies:
        copy.wait()


def preload(key_weight, value_weight):
    return pl.pallas_call(
        preload_kernel,
        out_shape=(pltpu.VMEM(key_weight.shape, BF16),) * 2,
        in_specs=[anywhere()] * 2,
        out_specs=(vmem(),) * 2,
        scratch_shapes=[pltpu.SemaphoreType.DMA((2,))],
        compiler_params=pltpu.CompilerParams(vmem_limit_bytes=2 * MIB),
        cost_estimate=pl.CostEstimate(flops=0, bytes_accessed=1024, transcendentals=0),
        name="preload",
    )(key_weight, value_weight)


def normalise(x_refs, gain_refs, normed):
    width = x_refs[0].shape[1]
    gains = [gain_refs[0][...].reshape(1, width).astype(F32)]
    gains += [far[BLOCK:, :].astype(F32)[0:1] for far in x_refs[3:]]
    gains += [gain_refs[1][...].reshape(1, width).astype(F32)]
    for block in range(2):
        rows = pl.ds(block * BLOCK, BLOCK)
        parts = [x_ref[rows, :] for x_ref in x_refs[:3]] + [x_refs[3 + block][:BLOCK, :]]
        total = jnp.zeros((BLOCK, 1), F32)
        for part in parts:
            floats = part.astype(F32)
            total += jnp.sum(floats * floats, axis=-1, keepdims=True)
        scale = lax.rsqrt(total * (1.0 / (4 * width)) + 1e-06)
        for slot, part in enumerate(parts):
            normed[slot, rows, :] = (part.astype(F32) * scale * gains[slot]).astype(BF16)


def project_kernel(part, *refs):
    refs = list(refs)
    if part == 0:
        x_refs = [refs.pop(0) for _ in range(5)]
        gain_refs = [refs.pop(0) for _ in range(2)]
    else:
        normed = refs.pop(0)
    weight_refs = [refs.pop(0) for _ in range(2)]
    mine_ref, away_ref = refs[0:2]
    if part == 0:
        normed = refs[2]
        normalise(x_refs, gain_refs, normed)
    width = normed.shape[2]
    columns = PART * TILE
    y = lax.axis_index("mp")
    core = place()[2]
    for half, out_ref in enumerate((away_ref, mine_ref)):
        column = pl.multiple_of((core ^ (1 - half)) * HALF + part * columns, columns)
        for which in range(2):
            product = jnp.zeros((ROWS, columns), F32)
            for slot in range(4):
                row = pl.multiple_of(((y + OFFSETS[slot]) & 3) * width, width)
                product += jnp.dot(
                    normed[slot],
                    weight_refs[which][pl.ds(row, width), pl.ds(column, columns)],
                    preferred_element_type=F32,
                )
            for block in range(2):
                for pair in range(PART):
                    tile = product[
                        block * BLOCK : (block + 1) * BLOCK, pair * TILE : (pair + 1) * TILE
                    ]
                    if which == 1:
                        tile = tile.T
                    out_ref[block, which, pair] = tile.astype(BF16)


def project(part, inputs, key_weight, value_weight):
    shapes = [jax.ShapeDtypeStruct((2, 2, PART, TILE, BLOCK), BF16)] * 2
    if part == 0:
        shapes.append(jax.ShapeDtypeStruct((4, ROWS, inputs[0].shape[1]), BF16))
    return pl.pallas_call(
        functools.partial(project_kernel, part),
        out_shape=tuple(shapes),
        in_specs=[vmem()] * (len(inputs) + 2),
        out_specs=(vmem(),) * len(shapes),
        compiler_params=pltpu.CompilerParams(vmem_limit_bytes=12 * MIB),
        cost_estimate=pl.CostEstimate(flops=0, bytes_accessed=1024, transcendentals=0),
        name="project",
    )(*inputs, key_weight, value_weight)


def spread(top):
    def rows(pair):
        a = top[2 * pair : 2 * pair + 1]
        b = top[2 * pair + 1 : 2 * pair + 2]
        return jnp.concatenate(
            [
                jnp.broadcast_to(a, (HD, QTOK)),
                jnp.broadcast_to(b, (HD, QTOK)),
                jnp.broadcast_to(a, (8, QTOK)),
                jnp.broadcast_to(b, (8, QTOK)),
            ],
            axis=0,
        )

    return rows


def attend_kernel(part, slots, *refs):
    refs = list(refs)
    take = lambda n: [refs.pop(0) for _ in range(n)]
    wanted = refs.pop(0)
    q_hbm, kv_hbm = take(len(slots)), take(4)
    if part:
        early_out, early_stats = take(2)
        outs = take(2 * len(slots))
    else:
        early_out, early_stats = take(2)
    qbuf, kvbuf, masked, scores, run_sums, run_tops, chosen, in_sems = take(8)
    x, z, core = place()
    columns = pl.ds(part * PART * TILE, PART * TILE)
    copies = []
    for number in range(len(slots)):
        copies.append(
            pltpu.make_async_copy(
                q_hbm[number].at[:, :, columns],
                qbuf.at[pl.ds(2 * number, 2)],
                in_sems.at[4 + number],
            )
        )
    for t in range(4):
        copies.append(
            pltpu.make_async_copy(kv_hbm[t], kvbuf.at[pl.ds(2 * t, 2)], in_sems.at[t])
        )
    for copy in copies:
        copy.start()
    for copy in copies:
        copy.wait()

    def dp_index(along_x, offset, swapped):
        ex = jnp.where(along_x, (x + offset) & 3, x)
        ez = jnp.where(along_x, z, (z + offset) & 3)
        return (ex * 4 + ez) * 2 + (core ^ swapped)

    lane_half = lax.broadcasted_iota(jnp.int32, (QTOK, TILE), 1) // HD
    row = lax.broadcasted_iota(jnp.int32, (16, 2 * BLOCK), 0) // 8
    col = lax.broadcasted_iota(jnp.int32, (16, 2 * BLOCK), 1) // BLOCK
    ones = jnp.where(row == col, 1.0, 0.0).astype(BF16)
    empty = jnp.zeros((HD, BLOCK), BF16)

    encoders = [dp_index(core == 0, offset, swapped) for offset in OFFSETS for swapped in range(2)]

    def question(index, carry):
        number = index >> 1
        offset, offset_slot = jnp.int32(OFFSETS[slots[0]]), jnp.int32(slots[0])
        for other in range(1, len(slots)):
            offset = jnp.where(number == other, OFFSETS[slots[other]], offset)
            offset_slot = jnp.where(number == other, slots[other], offset_slot)
        q_index = dp_index(core == 1, offset, index & 1)
        count = jnp.int32(0)
        for t in range(4):
            for swapped in range(2):
                local = wanted[q_index, encoders[2 * t + swapped]]
                chosen[count] = (t * 2 + swapped) * 2 + jnp.maximum(local, 0)
                count = count + jnp.where(local >= 0, 1, 0)
        for pair in range(PART):
            query = qbuf[index, :, pair * TILE : (pair + 1) * TILE]
            for head in range(2):
                masked[pair, head] = jnp.where(lane_half == head, query, jnp.zeros_like(query))

        @pl.when(count == 0)
        def _():
            run_sums[...] = jnp.zeros((PART, SUMS, QTOK), F32)
            run_tops[...] = jnp.full((8, QTOK), LOW, F32)

        chosen[count] = chosen[jnp.maximum(count - 1, 0)]

        def weigh(size):
            places = [chosen[step] for step in range(size)]
            live = (count == size).astype(BF16)
            rows = []
            for pair in range(PART):
                keys = [kvbuf[where >> 1, where & 1, 0, pair] for where in places]
                keys = jnp.concatenate(keys, axis=0)
                for head in range(2):
                    s = lax.dot_general(
                        keys,
                        masked[pair, head],
                        (((1,), (1,)), ((), ())),
                        preferred_element_type=F32,
                    )
                    rows.append(jnp.max(s, axis=0, keepdims=True))
                    scores[:size, pair, head] = s.reshape(size, BLOCK, QTOK)
            run_tops[...] = jnp.concatenate(rows + rows, axis=0)
            for pair in range(PART):
                left, probs = [], []
                for step, where in enumerate(places):
                    for head in range(2):
                        shifted = scores[step, pair, head] - rows[2 * pair + head]
                        probs.append(jnp.exp(shifted).astype(BF16))
                    values, unit = kvbuf[where >> 1, where & 1, 1, pair], ones
                    if step == size - 1:
                        values, unit = values * live, unit * live
                    left.append(
                        jnp.concatenate(
                            [
                                jnp.concatenate([values[:HD], empty], axis=1),
                                jnp.concatenate([empty, values[HD:]], axis=1),
                                unit,
                            ],
                            axis=0,
                        )
                    )
                run_sums[pair] = jnp.dot(
                    jnp.concatenate(left, axis=1),
                    jnp.concatenate(probs, axis=0),
                    preferred_element_type=F32,
                )

        for size in (2, 4, 6, 8):

            @pl.when((count + 1) >> 1 == size // 2)
            def _(size=size):
                weigh(size)

        tops = run_tops[...]
        totals = []
        finished = []
        for pair in range(PART):
            done = run_sums[pair]
            finished.append(done)
            totals += [done[TILE : TILE + 1], done[TILE + 8 : TILE + 9]]
        total = jnp.concatenate(totals, axis=0)
        some = total > 0.0
        safe = jnp.where(some, total, 1.0)
        inverse = spread(1.0 / safe)
        pieces = [(done * inverse(pair))[:TILE].astype(BF16) for pair, done in enumerate(finished)]
        stat = jnp.where(some, tops[: 2 * PART] + jnp.log(safe), LOW)
        if part == 0:
            early_out[index] = jnp.concatenate(pieces, axis=0)
            early_stats[index] = jnp.concatenate([stat, stat], axis=0)
            return carry
        early = 2 * offset_slot + (index & 1)
        rest = jnp.concatenate([early_stats[early][: 2 * PART], stat], axis=0)
        pieces = [early_out[early]] + pieces
        stats = []
        for _ in range(3):
            rounded = rest.astype(BF16).astype(F32)
            stats.append(rounded)
            rest = rest - rounded
        stats.append(jnp.zeros_like(rest))
        pieces.append(jnp.concatenate(stats, axis=0).astype(BF16))
        message = jnp.concatenate(pieces, axis=0)
        for other in range(2 * len(slots)):

            @pl.when(index == other)
            def _(other=other):
                outs[other][...] = message

        return carry

    lax.fori_loop(0, 2 * len(slots), question, 0)


def attend(part, wanted, queries, blocks, slots, early=()):
    count = 2 * len(slots)
    if part:
        out_shape = (jax.ShapeDtypeStruct((HALF + STAT, QTOK), BF16),) * count
    else:
        out_shape = (
            jax.ShapeDtypeStruct((count, PART * TILE, QTOK), BF16),
            jax.ShapeDtypeStruct((count, 8, QTOK), F32),
        )
    return pl.pallas_call(
        functools.partial(attend_kernel, part, slots),
        out_shape=out_shape,
        in_specs=[pl.BlockSpec(memory_space=pltpu.SMEM)]
        + [anywhere()] * (len(slots) + 4)
        + [vmem()] * len(early),
        out_specs=(vmem(),) * len(out_shape),
        scratch_shapes=[
            pltpu.VMEM((count, QTOK, PART * TILE), BF16),
            pltpu.VMEM((8, 2, 2, PART, TILE, BLOCK), BF16),
            pltpu.VMEM((PART, 2, QTOK, TILE), BF16),
            pltpu.VMEM((8, PART, 2, BLOCK, QTOK), F32),
            pltpu.VMEM((PART, SUMS, QTOK), F32),
            pltpu.VMEM((8, QTOK), F32),
            pltpu.SMEM((16,), jnp.int32),
            pltpu.SemaphoreType.DMA((4 + len(slots),)),
        ],
        compiler_params=pltpu.CompilerParams(vmem_limit_bytes=24 * MIB),
        cost_estimate=pl.CostEstimate(
            flops=count * 10**9, bytes_accessed=8 * MIB, transcendentals=0
        ),
        name="attend",
    )(wanted, *[queries[slot] for slot in slots], *blocks, *early)


def merged(refs):
    stats = []
    for ref in refs:
        stat = ref[HALF : HALF + STAT, :].astype(F32)
        stats.append(stat[0:8] + stat[8:16] + stat[16:24])
    top = functools.reduce(jnp.maximum, stats)
    weights = [jnp.exp(stat - top) for stat in stats]
    inverse = 1.0 / sum(weights)
    weights = [weight * inverse for weight in weights]
    heads = []
    for head in range(2 * PAIRS):
        heads.append(
            sum(
                ref[head * HD : (head + 1) * HD, :].astype(F32) * weight[head : head + 1]
                for ref, weight in zip(refs, weights)
            ).astype(BF16)
        )
    row = lax.broadcasted_iota(jnp.int32, (QTOK, QTOK), 0)
    col = lax.broadcasted_iota(jnp.int32, (QTOK, QTOK), 1)
    unit = jnp.where(row == col, 1.0, 0.0).astype(BF16)
    return lax.dot_general(
        unit,
        jnp.concatenate(heads, axis=0),
        (((1,), (1,)), ((), ())),
        preferred_element_type=F32,
    )


def merge_kernel(*refs):
    out_ref = refs[8]
    core = place()[2]
    for half in range(2):
        column = pl.multiple_of((core ^ half) * HALF, HALF)
        out_ref[:, pl.ds(column, HALF)] = merged(refs[4 * half : 4 * half + 4]).astype(BF16)


def merge(mine, away):
    return pl.pallas_call(
        merge_kernel,
        out_shape=jax.ShapeDtypeStruct((QTOK, 2 * HALF), BF16),
        in_specs=[vmem()] * 8,
        out_specs=vmem(),
        compiler_params=pltpu.CompilerParams(vmem_limit_bytes=16 * MIB),
        name="merge",
    )(*mine, *away)


def both_cores(mine, away):
    return jnp.concatenate([mine[None], send(away, CORE_SWAP)[None]], axis=0)


def local(block_states, norm_gain, key_weight, value_weight, queries, wanted):
    kv_ring = functools.partial(along_ring, first_along_x=True)
    q_ring = functools.partial(along_ring, first_along_x=False)
    core = place()[2]
    own = block_states.reshape(ROWS, block_states.shape[2])
    left, right = send(own, along_y(1)), send(own, along_y(-1))
    far_gain = send(norm_gain, along_y(2))
    other = send(queries, CORE_SWAP)
    halves = [lax.dynamic_slice_in_dim(each, core * HALF, HALF, 1)[None] for each in (queries, other)]
    q_pair = jnp.concatenate(halves, axis=0)
    q_far, q_right = send(q_pair, q_ring(2)), send(q_pair, q_ring(-1))
    gain_rows = jnp.broadcast_to(norm_gain[None], (16, norm_gain.shape[0]))
    key_weight, value_weight = preload(key_weight, value_weight)
    left, right, key_weight, value_weight = lax.optimization_barrier(
        (left, right, key_weight, value_weight)
    )
    far = [
        send(jnp.concatenate([left[:BLOCK], gain_rows], axis=0), along_y(1)),
        send(jnp.concatenate([right[BLOCK:], gain_rows], axis=0), along_y(-1)),
    ]
    q_left = send(lax.optimization_barrier((q_pair, left))[0], q_ring(1))
    q_far, q_right, far[0] = lax.optimization_barrier((q_far, q_right, far[0]))
    inputs = [own, left, right, *far, norm_gain, far_gain]
    *ready, normed = project(0, inputs, key_weight, value_weight)
    kv = gather(both_cores(*ready), kv_ring)
    normed, q_left = lax.optimization_barrier((normed, q_left))
    kv_late = gather(both_cores(*project(1, [normed], key_weight, value_weight)), kv_ring)
    slots_q = [q_pair, q_left, q_right, q_far]
    early = attend(0, wanted, slots_q, kv, (0, 1, 2, 3))
    mine, away = [], []
    for slots in ((3,), (1, 2), (0,)):
        outs = attend(1, wanted, slots_q, kv_late, slots, early)
        for number, slot in enumerate(slots):
            same, cross = outs[2 * number : 2 * number + 2]
            step = OFFSETS[slot]
            mine.append(send(same, q_ring(step)) if slot else same)
            away.append(send(cross, q_ring(step, cross=1)))
    return merge(mine, away)


def solution(mesh):
    return jax.shard_map(
        local,
        mesh=mesh,
        in_specs=(P("dp", None, "mp"), P("mp"), P(None, "mp"), P(None, "mp"), P("dp", "mp"), P()),
        out_specs=P("dp", "mp"),
        check_vma=False,
    )
```
